32 devices in a mesh: grp: 2 (over x), chan: 16 (over z, y, core).
Axes of the slice: x: 2, y: 2, z: 4, core: 2. Of those that a mesh axis runs over, the one named last changes fastest.
Arguments:
- voltages: int32 [512, 2, 2, 32, 1024], P(('grp', 'chan')), parts along dimension 0, may hold values from -127 to 127
- scales: int32 [512, 1024], P(('grp', 'chan')), parts along dimension 0, may hold values from 1 to 8
- feed_positions: float32 [3, 1024], replicated, may hold values from -8 to 8
- beam_directions: float32 [3, 128], replicated, may hold values from -1 to 1
- dm_trials: int32 [256], replicated, may hold values from 0 to 255, each once
Outputs:
- dedispersed: float32 [256, 32, 256], P(None, ('grp', 'chan')), parts along dimension 1
The draws below stay inside these ranges and needn't reach their ends.
There are 2 independent parts, one for each index of `grp`. The reference program is written for one: setup_inputs(seed, part) draws one part's arguments, and reference() takes and returns one part's arrays. A program takes and returns all parts, laid end to end along the dimension named above; an argument that names none is the same for every part. Nothing has to cross between parts.
Inputs may be any that keep to these rules, and one draw needn't show every extreme that they name: dm_trials holds each number of 0 to 255 once.
All inputs are finite; a program needn't handle non-finite values.
Results may differ from the reference program's by a relative error of at most 0.0046.
Values may be sent and summed in bfloat16 or wider, within the bound.
No kernel may reach another device: no remote copies, remote signals or barrier semaphores. Data moves between devices by JAX's collectives and lax.ppermute only.
A program may use at most 320 MiB of HBM per device.

```python
import math
import jax
import jax.numpy as jnp
from jax import lax

FEEDS = 1024
CH_DEV = 16
ND = 256
MAXD = 15
TV = 32
CHANNELS = 256
BEAMS = 128
TT = 16
BG = 8
BB = 16


def with_ends(values, own_key, low, largest):
    index_at = [jax.random.randint(jax.random.fold_in(own_key, axis), (), 0, length) for axis, length in enumerate(values.shape)]
    widest = values.shape.index(max(values.shape))
    next_to = index_at[:widest] + [(index_at[widest] + 1) % values.shape[widest]] + index_at[widest + 1:]
    return values.at[tuple(index_at)].set(low).at[tuple(next_to)].set(largest)


def setup_inputs(seed: int = 0, part: int = 0) -> dict:
    splits = jax.random.split(jax.random.key(seed), 6)
    part_splits = jax.random.split(jax.random.fold_in(splits[5], part), 6)
    voltages = with_ends(jax.random.randint(part_splits[0], (CHANNELS, 2, 2, TV, FEEDS), -127, 128), jax.random.fold_in(part_splits[0], 1), -127, 127).astype(jnp.int32)
    scales = with_ends(jax.random.randint(part_splits[1], (CHANNELS, FEEDS), 1, 9), jax.random.fold_in(part_splits[1], 1), 1, 8).astype(jnp.int32)
    feed_positions = jnp.clip(jax.random.uniform(splits[2], (3, FEEDS), jnp.float32, -8.0, 8.0), -8.0, 8.0)
    beam_directions = jnp.clip(jax.random.uniform(splits[3], (3, BEAMS), jnp.float32, -1.0, 1.0), -1.0, 1.0)
    dm_trials = jax.random.permutation(splits[4], ND).astype(jnp.int32)
    return {"voltages": voltages, "scales": scales, "feed_positions": feed_positions, "beam_directions": beam_directions, "dm_trials": dm_trials}


TWO_PI = 6.283185307179586
POWER_SCALE = 1.0 / 67108864.0

def geometry_delay(feed_positions, beam_directions):
    total = feed_positions[0][:, None] * beam_directions[0][None, :]
    total = total + feed_positions[1][:, None] * beam_directions[1][None, :]
    return total + feed_positions[2][:, None] * beam_directions[2][None, :]

def channel_flat(volt_chan, scale_chan, freq_chan, geometry):
    phase = TWO_PI * freq_chan * geometry
    scale_col = scale_chan.astype(jnp.float32)[:, None]
    weight_pair = jnp.concatenate([scale_col * jnp.cos(phase), scale_col * jnp.sin(phase)], axis=1).astype(jnp.bfloat16)
    row_block = volt_chan.astype(jnp.bfloat16).reshape(-1, volt_chan.shape[-1])
    product = jnp.dot(row_block, weight_pair, preferred_element_type=jnp.float32)
    beam_count = geometry.shape[1]
    product = product.reshape(2, 2, volt_chan.shape[2], 2, beam_count)
    real_part = product[0, :, :, 0] - product[1, :, :, 1]
    imag_part = product[0, :, :, 1] + product[1, :, :, 0]
    detected = real_part[0] * real_part[0] + imag_part[0] * imag_part[0] + (real_part[1] * real_part[1] + imag_part[1] * imag_part[1])
    detected = detected * POWER_SCALE
    return (detected - lax.optimization_barrier(jnp.mean(detected, axis=0, keepdims=True))).astype(jnp.bfloat16)

def delay_table(dm_trials, chan_total):
    chan_ids = jnp.arange(chan_total, dtype=jnp.int32)
    upper = jnp.int32(chan_total) + chan_ids
    sweeps = jnp.int32(256 * chan_total * chan_total) // (upper * upper) - jnp.int32(64)
    return dm_trials[:, None] * sweeps[None, :] * jnp.int32(MAXD + 1) // jnp.int32(ND * 192)

def reference(voltages, scales, feed_positions, beam_directions, dm_trials):
    geometry = geometry_delay(feed_positions, beam_directions)
    chan_ids = jnp.arange(CHANNELS, dtype=jnp.int32)
    base_ids = chan_ids - chan_ids % jnp.int32(CH_DEV)
    frequencies = base_ids.astype(jnp.float32) / CHANNELS + 1.0
    flat = lax.map(lambda items: channel_flat(items[0], items[1], items[2], geometry), (voltages, scales, frequencies))
    delays = delay_table(dm_trials, CHANNELS)
    extended = jnp.pad(flat, ((0, 0), (0, MAXD), (0, 0)))
    accumulate = jnp.zeros((ND, TV * BEAMS), jnp.float32)
    for shift_step in range(MAXD + 1):
        onehot = (delays == shift_step).astype(jnp.bfloat16)
        segment = extended[:, shift_step:shift_step + TV, :].reshape(CHANNELS, TV * BEAMS)
        accumulate = accumulate + jnp.dot(onehot, segment, preferred_element_type=jnp.float32)
    summed = accumulate * (1.0 / math.sqrt(CHANNELS))
    arranged = summed.reshape(ND, 2, TT, BG, BB).transpose(0, 1, 3, 2, 4)
    return arranged.reshape(ND, 2 * BG, TT * BB)
```

```python
import functools
import math

import numpy as np

import jax
import jax.numpy as jnp
from jax import lax
from jax.experimental import pallas as pl
from jax.experimental.pallas import tpu as pltpu
from jax.sharding import PartitionSpec as P

MAXD = 15
POWER_SCALE = 1.0 / 67108864.0
LANES = 128
CHANS = 16
OCTET = 8
VMEM_LIMIT = 48 * 1024 * 1024

SIN_TERMS = [(-1) ** k * (2 * math.pi) ** (2 * k + 1) / math.factorial(2 * k + 1) for k in range(5)]
COS_TERMS = [(-1) ** k * (2 * math.pi) ** (2 * k) / math.factorial(2 * k) for k in range(6)]


def horner(terms, square):
    total = jnp.full_like(square, terms[-1])
    for term in terms[-2::-1]:
        total = total * square + jnp.float32(term)
    return total


def cos_sin_turns(turns):
    quarters = jnp.round(turns * 4.0)
    rest = turns - quarters * 0.25
    square = rest * rest
    sine = horner(SIN_TERMS, square) * rest
    cosine = horner(COS_TERMS, square)
    which = quarters.astype(jnp.int32)
    swap = (which & 1) == 1
    base_cos = jnp.where(swap, sine, cosine)
    base_sin = jnp.where(swap, cosine, sine)
    cos_out = jnp.where(((which + 1) & 2) == 2, -base_cos, base_cos)
    sin_out = jnp.where((which & 2) == 2, -base_sin, base_sin)
    return cos_out, sin_out


def swap_lanes_and_list(tiles, width):
    count = len(tiles)
    lane = lax.broadcasted_iota(jnp.int32, tiles[0].shape, 1)
    tiles = list(tiles)
    step = count // 2
    while step >= 1:
        upper = ((lane // (step * width)) & 1) == 1
        for low in range(count):
            if low & step:
                continue
            a, b = tiles[low], tiles[low + step]
            tiles[low] = jnp.where(upper, pltpu.roll(b, step * width, 1), a)
            tiles[low + step] = jnp.where(upper, b, pltpu.roll(a, LANES - step * width, 1))
        step //= 2
    return tiles


def beam_kernel(chan_total, volt_hbm, scales_ref, pos_ref, dirs_ref, out_ref, volt, cosine, sine, power, sems):
    block = pl.program_id(0)
    copies = [pltpu.make_async_copy(volt_hbm.at[c], volt.at[c], sems.at[c]) for c in range(CHANS)]

    @pl.when(block == 0)
    def _():
        for copy in copies:
            copy.start()

    first_chan = lax.axis_index("chan") * CHANS
    frequency = first_chan.astype(jnp.float32) / chan_total + 1.0
    columns = jnp.transpose(jnp.concatenate([dirs_ref[...], jnp.zeros((5, LANES), jnp.float32)], axis=0))
    feeds = pos_ref.shape[1]
    for start in range(0, feeds, LANES):
        at = slice(start, start + LANES)
        geometry = pos_ref[0:1, at] * columns[:, 0:1]
        geometry = geometry + pos_ref[1:2, at] * columns[:, 1:2]
        geometry = geometry + pos_ref[2:3, at] * columns[:, 2:3]
        cosine[:, at], sine[:, at] = cos_sin_turns(frequency * geometry)

    window = volt.shape[3]
    for c in range(CHANS):
        @pl.when(block == 0)
        def _():
            copies[c].wait()

        rows = volt[c].reshape(4 * window, feeds).astype(jnp.float32).astype(jnp.bfloat16)
        scale = scales_ref[c : c + 1, :].astype(jnp.float32)
        weights = jnp.concatenate([(scale * cosine[...]).astype(jnp.bfloat16), (scale * sine[...]).astype(jnp.bfloat16)], axis=0)
        product = lax.dot_general(rows, weights, (((1,), (1,)), ((), ())), preferred_element_type=jnp.float32)
        half = 2 * window
        real = product[:half, :LANES] - product[half:, LANES:]
        imag = product[:half, LANES:] + product[half:, :LANES]
        both = real * real + imag * imag
        detected = both[:window] + both[window:]
        flat = detected - jnp.mean(detected, axis=0, keepdims=True)
        power[pl.ds(c, window, stride=CHANS), :] = flat

    zeros = jnp.zeros((2 * CHANS, LANES), jnp.bfloat16)
    for octet in range(window // OCTET):
        tiles = [power[(octet * OCTET + t) * CHANS : (octet * OCTET + t + 1) * CHANS, :] for t in range(OCTET)]
        tiles = swap_lanes_and_list(tiles, CHANS)
        for h in range(OCTET):
            tile = tiles[h].astype(jnp.bfloat16)
            out_ref[0, h, octet * CHANS : (octet + 1) * CHANS, :] = tile
            if octet >= 2:
                out_ref[1, h, (octet - 2) * CHANS : (octet - 1) * CHANS, :] = tile
    for h in range(OCTET):
        out_ref[1, h, 2 * CHANS :, :] = zeros


def beams(voltages, scales, feed_positions, beam_directions, chan_total):
    window, feeds = voltages.shape[3:]
    beam_count = beam_directions.shape[1]
    blocks = beam_count // LANES
    return pl.pallas_call(
        functools.partial(beam_kernel, chan_total),
        grid=(blocks,),
        in_specs=[
            pl.BlockSpec(memory_space=pl.ANY),
            pl.BlockSpec((CHANS, feeds), lambda i: (0, 0)),
            pl.BlockSpec((3, feeds), lambda i: (0, 0)),
            pl.BlockSpec((3, LANES), lambda i: (0, i)),
        ],
        out_specs=pl.BlockSpec((2, OCTET, 4 * CHANS, LANES), lambda i: (0, i, 0, 0)),
        out_shape=jax.ShapeDtypeStruct((2, blocks * OCTET, 4 * CHANS, LANES), jnp.bfloat16),
        scratch_shapes=[
            pltpu.VMEM(voltages.shape, jnp.int32),
            pltpu.VMEM((LANES, feeds), jnp.float32),
            pltpu.VMEM((LANES, feeds), jnp.float32),
            pltpu.VMEM((window * CHANS, LANES), jnp.float32),
            pltpu.SemaphoreType.DMA((CHANS,)),
        ],
        compiler_params=pltpu.CompilerParams(vmem_limit_bytes=VMEM_LIMIT),
        name="beams",
    )(voltages, scales, feed_positions, beam_directions)


def dedisperse_kernel(scaling, divisor, arrived_ref, sweeps_ref, dm_ref, out_ref, masks, pieces):
    trials = out_ref.shape[0]
    part = pl.program_id(0)
    delays = (dm_ref[...] * sweeps_ref[...]) // divisor
    depth = delays.shape[1]
    tiles = [arrived_ref[:, o * CHANS : (o + 1) * CHANS, :].reshape(depth, LANES).astype(jnp.float32) for o in range(4)]
    lane = lax.broadcasted_iota(jnp.int32, (depth, LANES), 1)
    for r in range(OCTET):
        if r == 0:
            moved = tiles[:3]
        else:
            rolled = [pltpu.roll(tile, LANES - r * CHANS, 1) for tile in tiles]
            moved = [jnp.where(lane < LANES - r * CHANS, rolled[o], rolled[o + 1]) for o in range(3)]
        moved = [tile.astype(jnp.bfloat16) for tile in moved]
        for a in range(2):
            shift = OCTET * a + r
            masks[:, shift * depth : (shift + 1) * depth] = jnp.where(delays == shift, 1.0, 0.0).astype(jnp.bfloat16)
            pieces[shift * depth : (shift + 1) * depth, :LANES] = moved[a]
            pieces[shift * depth : (shift + 1) * depth, LANES:] = moved[a + 1]
    total = jnp.dot(masks[...], pieces[...], preferred_element_type=jnp.float32) * scaling

    @pl.when(part == 0)
    def _():
        out_ref[...] = total

    @pl.when(part > 0)
    def _():
        out_ref[...] += total


def dedisperse(arrived, dm_trials, chan_total):
    sources = arrived.shape[0]
    trials = dm_trials.shape[0]
    ids = np.arange(chan_total, dtype=np.int64)
    sweeps = ((256 * chan_total * chan_total) // ((chan_total + ids) ** 2) - 64).astype(np.int32)
    group = min(sources, 16)
    depth = group * CHANS
    scaling = POWER_SCALE / math.sqrt(chan_total)
    divisor = trials * 192 // (MAXD + 1)
    return pl.pallas_call(
        functools.partial(dedisperse_kernel, scaling, divisor),
        grid=(sources // group,),
        in_specs=[
            pl.BlockSpec((group, 4 * CHANS, LANES), lambda i: (i, 0, 0)),
            pl.BlockSpec((1, depth), lambda i: (0, i)),
            pl.BlockSpec((trials, 1), lambda i: (0, 0)),
        ],
        out_specs=pl.BlockSpec((trials, 2 * LANES), lambda i: (0, 0)),
        out_shape=jax.ShapeDtypeStruct((trials, 2 * LANES), jnp.float32),
        scratch_shapes=[
            pltpu.VMEM((trials, (MAXD + 1) * depth), jnp.bfloat16),
            pltpu.VMEM(((MAXD + 1) * depth, 2 * LANES), jnp.bfloat16),
        ],
        compiler_params=pltpu.CompilerParams(vmem_limit_bytes=VMEM_LIMIT),
        name="dedisperse",
    )(arrived, jnp.asarray(sweeps)[None, :], dm_trials[:, None])


def local(voltages, scales, feed_positions, beam_directions, dm_trials):
    groups = lax.axis_size("chan")
    chan_total = groups * voltages.shape[0]
    outgoing = beams(voltages, scales, feed_positions, beam_directions, chan_total)
    outgoing = outgoing.reshape(groups, 4 * CHANS, LANES)
    arrived = lax.all_to_all(outgoing, "chan", split_axis=0, concat_axis=0, tiled=True)
    result = dedisperse(arrived, dm_trials, chan_total)
    return result[:, None, :]


def solution(mesh):
    return jax.shard_map(
        local,
        mesh=mesh,
        in_specs=(
            P(("grp", "chan"), None, None, None, None),
            P(("grp", "chan"), None),
            P(),
            P(),
            P(),
        ),
        out_specs=P(None, ("grp", "chan"), None),
        check_vma=False,
    )
```

```python
import functools
import math

import numpy as np

import jax
import jax.numpy as jnp
from jax import lax
from jax.experimental import pallas as pl
from jax.experimental.pallas import tpu as pltpu
from jax.sharding import PartitionSpec as P

MAXD = 15
POWER_SCALE = 1.0 / 67108864.0
LANES = 128
CHANS = 16
OCTET = 8
BATCHES = (4, 4, 4, 4)
DEPTH = 256
BEAM_VMEM = 40 * 1024 * 1024
VMEM_LIMIT = 24 * 1024 * 1024

SIN_TERMS = [(-1) ** k * (2 * math.pi) ** (2 * k + 1) / math.factorial(2 * k + 1) for k in range(5)]
COS_TERMS = [(-1) ** k * (2 * math.pi) ** (2 * k) / math.factorial(2 * k) for k in range(6)]


def horner(terms, square):
    total = jnp.full_like(square, terms[-1])
    for term in terms[-2::-1]:
        total = total * square + jnp.float32(term)
    return total


def cos_sin_turns(turns):
    quarters = jnp.round(turns * 4.0)
    rest = turns - quarters * 0.25
    square = rest * rest
    sine = horner(SIN_TERMS, square) * rest
    cosine = horner(COS_TERMS, square)
    which = quarters.astype(jnp.int32)
    swap = (which & 1) == 1
    base_cos = jnp.where(swap, sine, cosine)
    base_sin = jnp.where(swap, cosine, sine)
    cos_out = jnp.where(((which + 1) & 2) == 2, -base_cos, base_cos)
    sin_out = jnp.where((which & 2) == 2, -base_sin, base_sin)
    return cos_out, sin_out


def swap_lanes_and_list(tiles, width):
    count = len(tiles)
    lane = lax.broadcasted_iota(jnp.int32, tiles[0].shape, 1)
    tiles = list(tiles)
    step = count // 2
    while step >= 1:
        upper = ((lane // (step * width)) & 1) == 1
        for low in range(count):
            if low & step:
                continue
            a, b = tiles[low], tiles[low + step]
            tiles[low] = jnp.where(upper, pltpu.roll(b, step * width, 1), a)
            tiles[low + step] = jnp.where(upper, b, pltpu.roll(a, LANES - step * width, 1))
        step //= 2
    return tiles


def in_first_block(blocks, action):
    if blocks == 1:
        action()
    else:
        pl.when(pl.program_id(0) == 0)(action)


def channel_product(volt, c, scale_columns, cosine, sine, window, feeds):
    total = None
    for low in range(0, feeds, DEPTH):
        at = slice(low, low + DEPTH)
        rows = volt[c, :, :, :, at].reshape(4 * window, DEPTH).astype(jnp.float32).astype(jnp.bfloat16)
        scale = jnp.broadcast_to(scale_columns[at, c : c + 1], (DEPTH, LANES)).astype(jnp.float32)
        weights = jnp.concatenate([(scale * cosine[at, :]).astype(jnp.bfloat16), (scale * sine[at, :]).astype(jnp.bfloat16)], axis=1)
        part = jnp.dot(rows, weights, preferred_element_type=jnp.float32)
        total = part if total is None else total + part
    return total


def beam_kernel(chan_total, blocks, volt_hbm, scales_hbm, pos_hbm, dirs_hbm, out_ref, volt, scales, pos, dirs, cosine, sine, power, sems, small_sems):
    edges = [sum(BATCHES[:k]) for k in range(len(BATCHES) + 1)]
    small = [
        pltpu.make_async_copy(source, target, small_sems.at[k])
        for k, (source, target) in enumerate(((pos_hbm, pos), (dirs_hbm, dirs), (scales_hbm, scales)))
    ]
    copies = [
        pltpu.make_async_copy(volt_hbm.at[low:high], volt.at[low:high], sems.at[k])
        for k, (low, high) in enumerate(zip(edges, edges[1:]))
    ]

    def start_all():
        for copy in small + copies:
            copy.start()
        for copy in small:
            copy.wait()

    in_first_block(blocks, start_all)

    first_chan = lax.axis_index("chan") * CHANS
    frequency = first_chan.astype(jnp.float32) / chan_total + 1.0
    feeds = pos.shape[1]
    places = jnp.transpose(jnp.concatenate([pos[...], jnp.zeros((5, feeds), jnp.float32)], axis=0))
    if blocks == 1:
        beam_rows = dirs[...]
    else:
        beam_rows = dirs[:, pl.ds(pl.multiple_of(pl.program_id(0) * LANES, LANES), LANES)]
    geometry = places[:, 0:1] * beam_rows[0:1, :]
    geometry = geometry + places[:, 1:2] * beam_rows[1:2, :]
    geometry = geometry + places[:, 2:3] * beam_rows[2:3, :]
    cosine[...], sine[...] = cos_sin_turns(frequency * geometry)
    scale_columns = jnp.transpose(scales[...].astype(jnp.float32)).astype(jnp.bfloat16)

    window = volt.shape[3]
    for c in range(CHANS):
        if c in edges:
            in_first_block(blocks, copies[edges.index(c)].wait)

        product = channel_product(volt, c, scale_columns, cosine, sine, window, feeds)
        half = 2 * window
        real = product[:half, :LANES] - product[half:, LANES:]
        imag = product[:half, LANES:] + product[half:, :LANES]
        both = real * real + imag * imag
        detected = both[:window] + both[window:]
        flat = detected - jnp.mean(detected, axis=0, keepdims=True)
        power[pl.ds(c, window, stride=CHANS), :] = flat

    zeros = jnp.zeros((2 * CHANS, LANES), jnp.bfloat16)
    for octet in range(window // OCTET):
        tiles = [power[(octet * OCTET + t) * CHANS : (octet * OCTET + t + 1) * CHANS, :] for t in range(OCTET)]
        tiles = swap_lanes_and_list(tiles, CHANS)
        for h in range(OCTET):
            tile = tiles[h].astype(jnp.bfloat16)
            out_ref[0, h, octet * CHANS : (octet + 1) * CHANS, :] = tile
            if octet >= 2:
                out_ref[1, h, (octet - 2) * CHANS : (octet - 1) * CHANS, :] = tile
    for h in range(OCTET):
        out_ref[1, h, 2 * CHANS :, :] = zeros


def beams(voltages, scales, feed_positions, beam_directions, chan_total):
    window, feeds = voltages.shape[3:]
    beam_count = beam_directions.shape[1]
    blocks = beam_count // LANES
    return pl.pallas_call(
        functools.partial(beam_kernel, chan_total, blocks),
        grid=(blocks,),
        in_specs=[
            pl.BlockSpec(memory_space=pl.ANY),
            pl.BlockSpec(memory_space=pl.ANY),
            pl.BlockSpec(memory_space=pl.ANY),
            pl.BlockSpec(memory_space=pl.ANY),
        ],
        out_specs=pl.BlockSpec((2, OCTET, 4 * CHANS, LANES), lambda i: (0, i, 0, 0)),
        out_shape=jax.ShapeDtypeStruct((2, blocks * OCTET, 4 * CHANS, LANES), jnp.bfloat16),
        scratch_shapes=[
            pltpu.VMEM(voltages.shape, jnp.int32),
            pltpu.VMEM(scales.shape, jnp.int32),
            pltpu.VMEM(feed_positions.shape, jnp.float32),
            pltpu.VMEM(beam_directions.shape, jnp.float32),
            pltpu.VMEM((feeds, LANES), jnp.float32),
            pltpu.VMEM((feeds, LANES), jnp.float32),
            pltpu.VMEM((window * CHANS, LANES), jnp.float32),
            pltpu.SemaphoreType.DMA((len(BATCHES),)),
            pltpu.SemaphoreType.DMA((3,)),
        ],
        compiler_params=pltpu.CompilerParams(vmem_limit_bytes=BEAM_VMEM),
        name="beams",
    )(*(pltpu.with_memory_space_constraint(x, pltpu.HBM) for x in (voltages, scales, feed_positions, beam_directions)))


def dedisperse_kernel(scaling, divisor, arrived_ref, sweeps_ref, dm_ref, out_ref, masks, pieces):
    trials = out_ref.shape[0]
    part = pl.program_id(0)
    product = (dm_ref[...] * sweeps_ref[...]).astype(jnp.float32)
    delays = jnp.floor((product + 0.5) * (1.0 / divisor))
    depth = delays.shape[1]
    tiles = [arrived_ref[:, o * CHANS : (o + 1) * CHANS, :].reshape(depth, LANES).astype(jnp.float32) for o in range(4)]
    lane = lax.broadcasted_iota(jnp.int32, (depth, LANES), 1)
    for r in range(OCTET):
        if r == 0:
            moved = tiles[:3]
        else:
            rolled = [pltpu.roll(tile, LANES - r * CHANS, 1) for tile in tiles]
            moved = [jnp.where(lane < LANES - r * CHANS, rolled[o], rolled[o + 1]) for o in range(3)]
        moved = [tile.astype(jnp.bfloat16) for tile in moved]
        for a in range(2):
            shift = OCTET * a + r
            masks[:, shift * depth : (shift + 1) * depth] = jnp.where(delays == shift, 1.0, 0.0).astype(jnp.bfloat16)
            pieces[shift * depth : (shift + 1) * depth, :LANES] = moved[a]
            pieces[shift * depth : (shift + 1) * depth, LANES:] = moved[a + 1]
    total = jnp.dot(masks[...], pieces[...], preferred_element_type=jnp.float32) * scaling

    @pl.when(part == 0)
    def _():
        out_ref[:, 0, :] = total

    @pl.when(part > 0)
    def _():
        out_ref[:, 0, :] += total


def dedisperse(arrived, dm_trials, chan_total):
    sources = arrived.shape[0]
    trials = dm_trials.shape[0]
    ids = np.arange(chan_total, dtype=np.int64)
    sweeps = ((256 * chan_total * chan_total) // ((chan_total + ids) ** 2) - 64).astype(np.int32)
    group = min(sources, 16)
    depth = group * CHANS
    scaling = POWER_SCALE / math.sqrt(chan_total)
    divisor = trials * 192 // (MAXD + 1)
    return pl.pallas_call(
        functools.partial(dedisperse_kernel, scaling, divisor),
        grid=(sources // group,),
        in_specs=[
            pl.BlockSpec((group, 4 * CHANS, LANES), lambda i: (i, 0, 0)),
            pl.BlockSpec((1, depth), lambda i: (0, i)),
            pl.BlockSpec((trials, 1), lambda i: (0, 0)),
        ],
        out_specs=pl.BlockSpec((trials, 1, 2 * LANES), lambda i: (0, 0, 0)),
        out_shape=jax.ShapeDtypeStruct((trials, 1, 2 * LANES), jnp.float32),
        scratch_shapes=[
            pltpu.VMEM((trials, (MAXD + 1) * depth), jnp.bfloat16),
            pltpu.VMEM(((MAXD + 1) * depth, 2 * LANES), jnp.bfloat16),
        ],
        compiler_params=pltpu.CompilerParams(vmem_limit_bytes=VMEM_LIMIT),
        name="dedisperse",
    )(arrived, jnp.asarray(sweeps)[None, :], dm_trials[:, None])


def local(voltages, scales, feed_positions, beam_directions, dm_trials):
    groups = lax.axis_size("chan")
    chan_total = groups * voltages.shape[0]
    outgoing = beams(voltages, scales, feed_positions, beam_directions, chan_total)
    outgoing = outgoing.reshape(groups, 4 * CHANS, LANES)
    arrived = lax.all_to_all(outgoing, "chan", split_axis=0, concat_axis=0, tiled=True)
    return dedisperse(arrived, dm_trials, chan_total)


def solution(mesh):
    return jax.shard_map(
        local,
        mesh=mesh,
        in_specs=(
            P(("grp", "chan"), None, None, None, None),
            P(("grp", "chan"), None),
            P(),
            P(),
            P(),
        ),
        out_specs=P(None, ("grp", "chan"), None),
        check_vma=False,
    )
```

```python
import functools
import math

import numpy as np

import jax
import jax.numpy as jnp
from jax import lax
from jax.experimental import pallas as pl
from jax.experimental.pallas import tpu as pltpu
from jax.sharding import PartitionSpec as P

MAXD = 15
POWER_SCALE = 1.0 / 67108864.0
LANES = 128
CHANS = 16
OCTET = 8
BATCHES = (5, 6, 5)
DEPTH = 256
EARLY = 1
BEAM_VMEM = 40 * 1024 * 1024
VMEM_LIMIT = 24 * 1024 * 1024

SIN_TERMS = [(-1) ** k * (2 * math.pi) ** (2 * k + 1) / math.factorial(2 * k + 1) for k in range(5)]
COS_TERMS = [(-1) ** k * (2 * math.pi) ** (2 * k) / math.factorial(2 * k) for k in range(6)]


def horner(terms, square):
    total = jnp.full_like(square, terms[-1])
    for term in terms[-2::-1]:
        total = total * square + jnp.float32(term)
    return total


def cos_sin_turns(turns):
    quarters = jnp.round(turns * 4.0)
    rest = turns - quarters * 0.25
    square = rest * rest
    sine = horner(SIN_TERMS, square) * rest
    cosine = horner(COS_TERMS, square)
    which = quarters.astype(jnp.int32)
    swap = (which & 1) == 1
    base_cos = jnp.where(swap, sine, cosine)
    base_sin = jnp.where(swap, cosine, sine)
    cos_out = jnp.where(((which + 1) & 2) == 2, -base_cos, base_cos)
    sin_out = jnp.where((which & 2) == 2, -base_sin, base_sin)
    return cos_out, sin_out


def swap_lanes_and_list(tiles, width):
    count = len(tiles)
    lane = lax.broadcasted_iota(jnp.int32, tiles[0].shape, 1)
    tiles = list(tiles)
    step = count // 2
    while step >= 1:
        upper = ((lane // (step * width)) & 1) == 1
        for low in range(count):
            if low & step:
                continue
            a, b = tiles[low], tiles[low + step]
            tiles[low] = jnp.where(upper, pltpu.roll(b, step * width, 1), a)
            tiles[low + step] = jnp.where(upper, b, pltpu.roll(a, LANES - step * width, 1))
        step //= 2
    return tiles


def in_first_block(blocks, action):
    if blocks == 1:
        action()
    else:
        pl.when(pl.program_id(0) == 0)(action)


def channel_product(volt, c, scale_columns, cosine, sine, window, feeds):
    total = None
    for low in range(0, feeds, DEPTH):
        at = slice(low, low + DEPTH)
        rows = volt[c, :, :, :, at].reshape(4 * window, DEPTH).astype(jnp.float32).astype(jnp.bfloat16)
        scale = jnp.broadcast_to(scale_columns[at, c : c + 1], (DEPTH, LANES)).astype(jnp.float32)
        weights = jnp.concatenate([(scale * cosine[at, :]).astype(jnp.bfloat16), (scale * sine[at, :]).astype(jnp.bfloat16)], axis=1)
        part = jnp.dot(rows, weights, preferred_element_type=jnp.float32)
        total = part if total is None else total + part
    return total


def beam_kernel(chan_total, blocks, volt_hbm, scales_hbm, pos_hbm, dirs_hbm, out_hbm, volt, scales, pos, dirs, cosine, sine, power, stage, sems, small_sems, out_sems):
    edges = [sum(BATCHES[:k]) for k in range(len(BATCHES) + 1)]
    small = [
        pltpu.make_async_copy(source, target, small_sems.at[k])
        for k, (source, target) in enumerate(((pos_hbm, pos), (dirs_hbm, dirs), (scales_hbm, scales)))
    ]
    copies = [
        pltpu.make_async_copy(volt_hbm.at[low:high], volt.at[low:high], sems.at[k])
        for k, (low, high) in enumerate(zip(edges, edges[1:]))
    ]

    first_row = 0 if blocks == 1 else pl.program_id(0) * OCTET

    def leave(source, group, octet):
        target = out_hbm.at[group, pl.ds(first_row, OCTET), octet * CHANS : (octet + 1) * CHANS, :]
        return pltpu.make_async_copy(source, target, out_sems.at[4 * group + octet])

    leaving = [[leave(stage.at[octet], 0, octet)] for octet in range(4)]
    for octet in range(2):
        leaving[2 + octet].append(leave(stage.at[2 + octet], 1, octet))
        leaving[octet].append(leave(stage.at[4], 1, 2 + octet))

    def start_all():
        for copy in small + copies[:EARLY]:
            copy.start()
        for copy in small:
            copy.wait()
        for copy in copies[EARLY:]:
            copy.start()

    in_first_block(blocks, start_all)

    stage[4] = jnp.zeros((OCTET, CHANS, LANES), jnp.bfloat16)
    first_chan = lax.axis_index("chan") * CHANS
    frequency = first_chan.astype(jnp.float32) / chan_total + 1.0
    feeds = pos.shape[1]
    places = jnp.transpose(jnp.concatenate([pos[...], jnp.zeros((5, feeds), jnp.float32)], axis=0))
    if blocks == 1:
        beam_rows = dirs[...]
    else:
        beam_rows = dirs[:, pl.ds(pl.multiple_of(pl.program_id(0) * LANES, LANES), LANES)]
    geometry = places[:, 0:1] * beam_rows[0:1, :]
    geometry = geometry + places[:, 1:2] * beam_rows[1:2, :]
    geometry = geometry + places[:, 2:3] * beam_rows[2:3, :]
    cosine[...], sine[...] = cos_sin_turns(frequency * geometry)
    scale_columns = jnp.transpose(scales[...].astype(jnp.float32)).astype(jnp.bfloat16)

    window = volt.shape[3]
    for c in range(CHANS):
        if c in edges:
            in_first_block(blocks, copies[edges.index(c)].wait)

        product = channel_product(volt, c, scale_columns, cosine, sine, window, feeds)
        half = 2 * window
        real = product[:half, :LANES] - product[half:, LANES:]
        imag = product[:half, LANES:] + product[half:, :LANES]
        both = real * real + imag * imag
        detected = both[:window] + both[window:]
        flat = detected - jnp.mean(detected, axis=0, keepdims=True)
        power[pl.ds(c, window, stride=CHANS), :] = flat

    for octet in range(window // OCTET):
        tiles = [power[(octet * OCTET + t) * CHANS : (octet * OCTET + t + 1) * CHANS, :] for t in range(OCTET)]
        tiles = swap_lanes_and_list([tile.astype(jnp.bfloat16) for tile in tiles], CHANS)
        for h in range(OCTET):
            stage[octet, h] = tiles[h]
        for copy in leaving[octet]:
            copy.start()
    for copy in sum(leaving, []):
        copy.wait()


def beams(voltages, scales, feed_positions, beam_directions, chan_total):
    window, feeds = voltages.shape[3:]
    beam_count = beam_directions.shape[1]
    blocks = beam_count // LANES
    return pl.pallas_call(
        functools.partial(beam_kernel, chan_total, blocks),
        grid=(blocks,),
        in_specs=[
            pl.BlockSpec(memory_space=pl.ANY),
            pl.BlockSpec(memory_space=pl.ANY),
            pl.BlockSpec(memory_space=pl.ANY),
            pl.BlockSpec(memory_space=pl.ANY),
        ],
        out_specs=pl.BlockSpec(memory_space=pl.ANY),
        out_shape=jax.ShapeDtypeStruct((2, blocks * OCTET, 4 * CHANS, LANES), jnp.bfloat16),
        scratch_shapes=[
            pltpu.VMEM(voltages.shape, jnp.int32),
            pltpu.VMEM(scales.shape, jnp.int32),
            pltpu.VMEM(feed_positions.shape, jnp.float32),
            pltpu.VMEM(beam_directions.shape, jnp.float32),
            pltpu.VMEM((feeds, LANES), jnp.float32),
            pltpu.VMEM((feeds, LANES), jnp.float32),
            pltpu.VMEM((window * CHANS, LANES), jnp.float32),
            pltpu.VMEM((5, OCTET, CHANS, LANES), jnp.bfloat16),
            pltpu.SemaphoreType.DMA((len(BATCHES),)),
            pltpu.SemaphoreType.DMA((3,)),
            pltpu.SemaphoreType.DMA((8,)),
        ],
        compiler_params=pltpu.CompilerParams(vmem_limit_bytes=BEAM_VMEM),
        name="beams",
    )(*(pltpu.with_memory_space_constraint(x, pltpu.HBM) for x in (voltages, scales, feed_positions, beam_directions)))


def masks_kernel(divisor, sweeps_ref, dm_ref, masks_ref):
    product = (dm_ref[...] * sweeps_ref[...]).astype(jnp.float32)
    delays = jnp.floor((product + 0.5) * (1.0 / divisor))
    depth = delays.shape[1]
    for shift in range(MAXD + 1):
        masks_ref[:, shift * depth : (shift + 1) * depth] = jnp.where(delays == shift, 1.0, 0.0).astype(jnp.bfloat16)


def shift_masks(dm_trials, chan_total, depth):
    trials = dm_trials.shape[0]
    ids = np.arange(chan_total, dtype=np.int64)
    sweeps = ((256 * chan_total * chan_total) // ((chan_total + ids) ** 2) - 64).astype(np.int32)
    return pl.pallas_call(
        functools.partial(masks_kernel, trials * 192 // (MAXD + 1)),
        grid=(chan_total // depth,),
        in_specs=[
            pl.BlockSpec((1, depth), lambda i: (0, i)),
            pl.BlockSpec((trials, 1), lambda i: (0, 0)),
        ],
        out_specs=pl.BlockSpec((trials, (MAXD + 1) * depth), lambda i: (0, i)),
        out_shape=jax.ShapeDtypeStruct((trials, (MAXD + 1) * chan_total), jnp.bfloat16),
        compiler_params=pltpu.CompilerParams(vmem_limit_bytes=VMEM_LIMIT),
        name="shift_masks",
    )(jnp.asarray(sweeps)[None, :], dm_trials[:, None])


def dedisperse_kernel(scaling, parts, arrived_ref, masks_ref, out_hbm, pieces, total, sem):
    part = pl.program_id(0)
    depth = arrived_ref.shape[0] * CHANS
    tiles = [arrived_ref[:, o * CHANS : (o + 1) * CHANS, :].reshape(depth, LANES) for o in range(4)]
    lane = lax.broadcasted_iota(jnp.int32, (depth, LANES), 1)
    for r in range(OCTET):
        if r == 0:
            moved = tiles[:3]
        else:
            rolled = [pltpu.roll(tile, LANES - r * CHANS, 1) for tile in tiles]
            moved = [jnp.where(lane < LANES - r * CHANS, rolled[o], rolled[o + 1]) for o in range(3)]
        for a in range(2):
            shift = OCTET * a + r
            pieces[shift * depth : (shift + 1) * depth, :LANES] = moved[a]
            pieces[shift * depth : (shift + 1) * depth, LANES:] = moved[a + 1]
    summed = jnp.dot(masks_ref[...], pieces[...], preferred_element_type=jnp.float32) * scaling
    if parts == 1:
        total[...] = summed
    else:
        total[...] = jnp.where(part == 0, 0.0, total[...]) + summed

    def leave():
        copy = pltpu.make_async_copy(total, out_hbm.at[:, 0, :], sem)
        copy.start()
        copy.wait()

    if parts == 1:
        leave()
    else:
        pl.when(part == parts - 1)(leave)


def dedisperse(arrived, masks, chan_total):
    sources = arrived.shape[0]
    trials = masks.shape[0]
    group = min(sources, 16)
    depth = group * CHANS
    scaling = POWER_SCALE / math.sqrt(chan_total)
    return pl.pallas_call(
        functools.partial(dedisperse_kernel, scaling, sources // group),
        grid=(sources // group,),
        in_specs=[
            pl.BlockSpec((group, 4 * CHANS, LANES), lambda i: (i, 0, 0)),
            pl.BlockSpec((trials, (MAXD + 1) * depth), lambda i: (0, i)),
        ],
        out_specs=pl.BlockSpec(memory_space=pl.ANY),
        out_shape=jax.ShapeDtypeStruct((trials, 1, 2 * LANES), jnp.float32),
        scratch_shapes=[
            pltpu.VMEM(((MAXD + 1) * depth, 2 * LANES), jnp.bfloat16),
            pltpu.VMEM((trials, 2 * LANES), jnp.float32),
            pltpu.SemaphoreType.DMA(()),
        ],
        compiler_params=pltpu.CompilerParams(vmem_limit_bytes=VMEM_LIMIT),
        name="dedisperse",
    )(arrived, masks)


def local(voltages, scales, feed_positions, beam_directions, dm_trials):
    groups = lax.axis_size("chan")
    chan_total = groups * voltages.shape[0]
    outgoing = beams(voltages, scales, feed_positions, beam_directions, chan_total)
    outgoing = outgoing.reshape(groups, 4 * CHANS, LANES)
    arrived = lax.all_to_all(outgoing, "chan", split_axis=0, concat_axis=0, tiled=True)
    masks = shift_masks(dm_trials, chan_total, min(groups, 16) * CHANS)
    return dedisperse(arrived, masks, chan_total)


def solution(mesh):
    return jax.shard_map(
        local,
        mesh=mesh,
        in_specs=(
            P(("grp", "chan"), None, None, None, None),
            P(("grp", "chan"), None),
            P(),
            P(),
            P(),
        ),
        out_specs=P(None, ("grp", "chan"), None),
        check_vma=False,
    )
```

```python
import functools
import math

import jax
import jax.numpy as jnp
from jax import lax
from jax.experimental import pallas as pl
from jax.experimental.pallas import tpu as pltpu
from jax.sharding import PartitionSpec as P

MAXD = 15
POWER_SCALE = 1.0 / 67108864.0
LANES = 128
CHANS = 16
OCTET = 8
BATCHES = (5, 6, 5)
DEPTH = 256
EARLY = 1
BEAM_VMEM = 40 * 1024 * 1024
VMEM_LIMIT = 24 * 1024 * 1024

SIN_TERMS = [(-1) ** k * (2 * math.pi) ** (2 * k + 1) / math.factorial(2 * k + 1) for k in range(5)]
COS_TERMS = [(-1) ** k * (2 * math.pi) ** (2 * k) / math.factorial(2 * k) for k in range(6)]


def horner(terms, square):
    total = jnp.full_like(square, terms[-1])
    for term in terms[-2::-1]:
        total = total * square + jnp.float32(term)
    return total


def cos_sin_turns(turns):
    quarters = jnp.round(turns * 4.0)
    rest = turns - quarters * 0.25
    square = rest * rest
    sine = horner(SIN_TERMS, square) * rest
    cosine = horner(COS_TERMS, square)
    which = quarters.astype(jnp.int32)
    swap = (which & 1) == 1
    base_cos = jnp.where(swap, sine, cosine)
    base_sin = jnp.where(swap, cosine, sine)
    cos_out = jnp.where(((which + 1) & 2) == 2, -base_cos, base_cos)
    sin_out = jnp.where((which & 2) == 2, -base_sin, base_sin)
    return cos_out, sin_out


def swap_lanes_and_list(tiles, width):
    count = len(tiles)
    lane = lax.broadcasted_iota(jnp.int32, tiles[0].shape, 1)
    tiles = list(tiles)
    step = count // 2
    while step >= 1:
        upper = ((lane // (step * width)) & 1) == 1
        for low in range(count):
            if low & step:
                continue
            a, b = tiles[low], tiles[low + step]
            tiles[low] = jnp.where(upper, pltpu.roll(b, step * width, 1), a)
            tiles[low + step] = jnp.where(upper, b, pltpu.roll(a, LANES - step * width, 1))
        step //= 2
    return tiles


def in_first_block(blocks, action):
    if blocks == 1:
        action()
    else:
        pl.when(pl.program_id(0) == 0)(action)


def channel_product(volt, c, scale_columns, cosine, sine, window, feeds):
    total = None
    for low in range(0, feeds, DEPTH):
        at = slice(low, low + DEPTH)
        rows = volt[c, :, :, :, at].reshape(4 * window, DEPTH).astype(jnp.float32).astype(jnp.bfloat16)
        scale = jnp.broadcast_to(scale_columns[at, c : c + 1], (DEPTH, LANES)).astype(jnp.float32)
        weights = jnp.concatenate([(scale * cosine[at, :]).astype(jnp.bfloat16), (scale * sine[at, :]).astype(jnp.bfloat16)], axis=1)
        part = jnp.dot(rows, weights, preferred_element_type=jnp.float32)
        total = part if total is None else total + part
    return total


def write_delays(divisor, dm, delays_ref):
    trials, chan_total = delays_ref.shape
    upper = chan_total + lax.broadcasted_iota(jnp.int32, (1, chan_total), 1)
    sweeps = ((256 * chan_total * chan_total) // (upper * upper) - 64).astype(jnp.float32)
    column = jnp.transpose(jnp.broadcast_to(dm[...].astype(jnp.float32), (8, trials)))[:, 0:1]
    delays_ref[...] = jnp.floor((column * sweeps + 0.5) * (1.0 / divisor))


def beam_kernel(chan_total, blocks, divisor, volt_hbm, scales_hbm, pos_hbm, dirs_hbm, dm_hbm, out_ref, delays_ref, volt, scales, pos, dirs, dm, cosine, sine, power, sems, small_sems):
    edges = [sum(BATCHES[:k]) for k in range(len(BATCHES) + 1)]
    small = [
        pltpu.make_async_copy(source, target, small_sems.at[k])
        for k, (source, target) in enumerate(((pos_hbm, pos), (dirs_hbm, dirs), (scales_hbm, scales), (dm_hbm, dm)))
    ]
    copies = [
        pltpu.make_async_copy(volt_hbm.at[low:high], volt.at[low:high], sems.at[k])
        for k, (low, high) in enumerate(zip(edges, edges[1:]))
    ]

    def start_all():
        for copy in small + copies[:EARLY]:
            copy.start()
        for copy in small:
            copy.wait()
        for copy in copies[EARLY:]:
            copy.start()

    in_first_block(blocks, start_all)

    in_first_block(blocks, lambda: write_delays(divisor, dm, delays_ref))
    first_chan = lax.axis_index("chan") * CHANS
    frequency = first_chan.astype(jnp.float32) / chan_total + 1.0
    feeds = pos.shape[1]
    places = jnp.transpose(jnp.concatenate([pos[...], jnp.zeros((5, feeds), jnp.float32)], axis=0))
    if blocks == 1:
        beam_rows = dirs[...]
    else:
        beam_rows = dirs[:, pl.ds(pl.multiple_of(pl.program_id(0) * LANES, LANES), LANES)]
    geometry = places[:, 0:1] * beam_rows[0:1, :]
    geometry = geometry + places[:, 1:2] * beam_rows[1:2, :]
    geometry = geometry + places[:, 2:3] * beam_rows[2:3, :]
    cosine[...], sine[...] = cos_sin_turns(frequency * geometry)
    scale_columns = jnp.transpose(scales[...].astype(jnp.float32)).astype(jnp.bfloat16)

    window = volt.shape[3]
    for c in range(CHANS):
        if c in edges:
            in_first_block(blocks, copies[edges.index(c)].wait)

        product = channel_product(volt, c, scale_columns, cosine, sine, window, feeds)
        half = 2 * window
        real = product[:half, :LANES] - product[half:, LANES:]
        imag = product[:half, LANES:] + product[half:, :LANES]
        both = real * real + imag * imag
        detected = both[:window] + both[window:]
        flat = detected - jnp.mean(detected, axis=0, keepdims=True)
        power[pl.ds(c, window, stride=CHANS), :] = flat

    for octet in range(window // OCTET):
        tiles = [power[(octet * OCTET + t) * CHANS : (octet * OCTET + t + 1) * CHANS, :] for t in range(OCTET)]
        tiles = swap_lanes_and_list([tile.astype(jnp.bfloat16) for tile in tiles], CHANS)
        for h in range(OCTET):
            out_ref[0, h, octet * CHANS : (octet + 1) * CHANS, :] = tiles[h]
            if octet >= 2:
                out_ref[1, h, (octet - 2) * CHANS : (octet - 1) * CHANS, :] = tiles[h]
    for h in range(OCTET):
        out_ref[1, h, 2 * CHANS :, :] = jnp.zeros((2 * CHANS, LANES), jnp.bfloat16)


def beams(voltages, scales, feed_positions, beam_directions, dm_trials, chan_total):
    window, feeds = voltages.shape[3:]
    beam_count = beam_directions.shape[1]
    blocks = beam_count // LANES
    trials = dm_trials.shape[0]
    divisor = trials * 192 // (MAXD + 1)
    inputs = (voltages, scales, feed_positions, beam_directions, dm_trials[None, :])
    return pl.pallas_call(
        functools.partial(beam_kernel, chan_total, blocks, divisor),
        grid=(blocks,),
        in_specs=[pl.BlockSpec(memory_space=pl.ANY)] * len(inputs),
        out_specs=(
            pl.BlockSpec((2, OCTET, 4 * CHANS, LANES), lambda i: (0, i, 0, 0)),
            pl.BlockSpec((trials, chan_total), lambda i: (0, 0)),
        ),
        out_shape=(
            jax.ShapeDtypeStruct((2, blocks * OCTET, 4 * CHANS, LANES), jnp.bfloat16),
            jax.ShapeDtypeStruct((trials, chan_total), jnp.float32),
        ),
        scratch_shapes=[
            pltpu.VMEM(voltages.shape, jnp.int32),
            pltpu.VMEM(scales.shape, jnp.int32),
            pltpu.VMEM(feed_positions.shape, jnp.float32),
            pltpu.VMEM(beam_directions.shape, jnp.float32),
            pltpu.VMEM((1, trials), jnp.int32),
            pltpu.VMEM((feeds, LANES), jnp.float32),
            pltpu.VMEM((feeds, LANES), jnp.float32),
            pltpu.VMEM((window * CHANS, LANES), jnp.float32),
            pltpu.SemaphoreType.DMA((len(BATCHES),)),
            pltpu.SemaphoreType.DMA((len(inputs) - 1,)),
        ],
        compiler_params=pltpu.CompilerParams(vmem_limit_bytes=BEAM_VMEM),
        name="beams",
    )(*(pltpu.with_memory_space_constraint(x, pltpu.HBM) for x in inputs))


def dedisperse_kernel(scaling, parts, arrived_ref, delays_ref, out_hbm, total, sem):
    part = pl.program_id(0)
    depth = arrived_ref.shape[0] * CHANS
    delays = delays_ref[...]
    tiles = [arrived_ref[:, o * CHANS : (o + 1) * CHANS, :].reshape(depth, LANES) for o in range(4)]
    lane = lax.broadcasted_iota(jnp.int32, (depth, LANES), 1)
    summed = None
    for r in range(OCTET):
        if r == 0:
            moved = tiles[:3]
        else:
            rolled = [pltpu.roll(tile, LANES - r * CHANS, 1) for tile in tiles]
            moved = [jnp.where(lane < LANES - r * CHANS, rolled[o], rolled[o + 1]) for o in range(3)]
        for a in range(2):
            mask = jnp.where(delays == OCTET * a + r, 1.0, 0.0).astype(jnp.bfloat16)
            piece = jnp.concatenate([moved[a], moved[a + 1]], axis=1)
            product = jnp.dot(mask, piece, preferred_element_type=jnp.float32)
            summed = product if summed is None else summed + product
    summed = summed * scaling
    if parts == 1:
        total[...] = summed
    else:
        total[...] = jnp.where(part == 0, 0.0, total[...]) + summed

    def leave():
        copy = pltpu.make_async_copy(total, out_hbm.at[:, 0, :], sem)
        copy.start()
        copy.wait()

    if parts == 1:
        leave()
    else:
        pl.when(part == parts - 1)(leave)


def dedisperse(arrived, delays):
    sources = arrived.shape[0]
    trials, chan_total = delays.shape
    group = min(sources, 16)
    depth = group * CHANS
    scaling = POWER_SCALE / math.sqrt(chan_total)
    return pl.pallas_call(
        functools.partial(dedisperse_kernel, scaling, sources // group),
        grid=(sources // group,),
        in_specs=[
            pl.BlockSpec((group, 4 * CHANS, LANES), lambda i: (i, 0, 0)),
            pl.BlockSpec((trials, depth), lambda i: (0, i)),
        ],
        out_specs=pl.BlockSpec(memory_space=pl.ANY),
        out_shape=jax.ShapeDtypeStruct((trials, 1, 2 * LANES), jnp.float32),
        scratch_shapes=[
            pltpu.VMEM((trials, 2 * LANES), jnp.float32),
            pltpu.SemaphoreType.DMA(()),
        ],
        compiler_params=pltpu.CompilerParams(vmem_limit_bytes=VMEM_LIMIT),
        name="dedisperse",
    )(arrived, delays)


def local(voltages, scales, feed_positions, beam_directions, dm_trials):
    groups = lax.axis_size("chan")
    chan_total = groups * voltages.shape[0]
    outgoing, delays = beams(voltages, scales, feed_positions, beam_directions, dm_trials, chan_total)
    outgoing = outgoing.reshape(groups, 4 * CHANS, LANES)
    arrived = lax.all_to_all(outgoing, "chan", split_axis=0, concat_axis=0, tiled=True)
    return dedisperse(arrived, delays)


def solution(mesh):
    return jax.shard_map(
        local,
        mesh=mesh,
        in_specs=(
            P(("grp", "chan"), None, None, None, None),
            P(("grp", "chan"), None),
            P(),
            P(),
            P(),
        ),
        out_specs=P(None, ("grp", "chan"), None),
        check_vma=False,
    )
```

```python
import functools
import math

import jax
import jax.numpy as jnp
from jax import lax
from jax.experimental import pallas as pl
from jax.experimental.pallas import tpu as pltpu
from jax.sharding import PartitionSpec as P

MAXD = 15
POWER_SCALE = 1.0 / 67108864.0
LANES = 128
CHANS = 16
OCTET = 8
BATCHES = (5, 6, 5)
DEPTH = 256
BEAM_VMEM = 40 * 1024 * 1024
VMEM_LIMIT = 24 * 1024 * 1024

SIN_TERMS = (6.283184916, -41.34158923, 81.59994333, -76.61447253, 41.34288235, -12.47124353)
COS_TERMS = (0.9999999891, -19.7392045, 64.93911746, -85.45013953, 60.16763095, -25.96759925, 6.528658158)


def horner(terms, square):
    total = jnp.full_like(square, terms[-1])
    for term in terms[-2::-1]:
        total = total * square + jnp.float32(term)
    return total


def cos_sin_turns(turns):
    rest = turns - jnp.round(turns)
    square = rest * rest
    return horner(COS_TERMS, square), horner(SIN_TERMS, square) * rest


def swap_lanes_and_list(tiles, width):
    count = len(tiles)
    lane = lax.broadcasted_iota(jnp.int32, tiles[0].shape, 1)
    tiles = list(tiles)
    step = count // 2
    while step >= 1:
        upper = ((lane // (step * width)) & 1) == 1
        for low in range(count):
            if low & step:
                continue
            a, b = tiles[low], tiles[low + step]
            tiles[low] = jnp.where(upper, pltpu.roll(b, step * width, 1), a)
            tiles[low + step] = jnp.where(upper, b, pltpu.roll(a, LANES - step * width, 1))
        step //= 2
    return tiles


def in_first_block(blocks, action):
    if blocks == 1:
        action()
    else:
        pl.when(pl.program_id(0) == 0)(action)


def channel_product(volt, c, scale_columns, cosine, sine, window, feeds):
    total = None
    for low in range(0, feeds, DEPTH):
        at = slice(low, low + DEPTH)
        rows = volt[c, :, :, :, at].reshape(4 * window, DEPTH).astype(jnp.float32).astype(jnp.bfloat16)
        scale = jnp.broadcast_to(scale_columns[at, c : c + 1], (DEPTH, LANES)).astype(jnp.float32)
        weights = jnp.concatenate([(scale * cosine[at, :]).astype(jnp.bfloat16), (scale * sine[at, :]).astype(jnp.bfloat16)], axis=1)
        part = jnp.dot(rows, weights, preferred_element_type=jnp.float32)
        total = part if total is None else total + part
    return total


def three_parts(rows):
    rest = jnp.concatenate([rows, jnp.zeros((5, rows.shape[1]), jnp.float32)], axis=0)
    parts = []
    for _ in range(3):
        parts.append(rest.astype(jnp.bfloat16).astype(jnp.float32))
        rest = rest - parts[-1]
    return parts


def write_delays(divisor, dm, delays_ref):
    trials, chan_total = delays_ref.shape
    upper = chan_total + lax.broadcasted_iota(jnp.int32, (1, chan_total), 1)
    sweeps = ((256 * chan_total * chan_total) // (upper * upper) - 64).astype(jnp.float32)
    column = jnp.transpose(jnp.broadcast_to(dm[...].astype(jnp.float32), (8, trials)))[:, 0:1]
    delays_ref[...] = jnp.floor((column * sweeps + 0.5) * (1.0 / divisor))


def beam_kernel(chan_total, blocks, divisor, volt_hbm, scales_hbm, pos_hbm, dirs_hbm, dm_hbm, out_ref, delays_ref, volt, scales, pos, dirs, dm, cosine, sine, power, sems, small_sems):
    edges = [sum(BATCHES[:k]) for k in range(len(BATCHES) + 1)]
    small = [
        pltpu.make_async_copy(source, target, small_sems.at[k])
        for k, (source, target) in enumerate(((pos_hbm, pos), (dirs_hbm, dirs), (scales_hbm, scales), (dm_hbm, dm)))
    ]
    copies = [
        pltpu.make_async_copy(volt_hbm.at[low:high], volt.at[low:high], sems.at[k])
        for k, (low, high) in enumerate(zip(edges, edges[1:]))
    ]

    def start_all():
        for copy in small:
            copy.start(priority=0)
        for copy in copies:
            copy.start(priority=1)
        for copy in small:
            copy.wait()

    in_first_block(blocks, start_all)

    in_first_block(blocks, lambda: write_delays(divisor, dm, delays_ref))
    first_chan = lax.axis_index("chan") * CHANS
    frequency = first_chan.astype(jnp.float32) / chan_total + 1.0
    feeds = pos.shape[1]
    if blocks == 1:
        beam_rows = dirs[...]
    else:
        beam_rows = dirs[:, pl.ds(pl.multiple_of(pl.program_id(0) * LANES, LANES), LANES)]
    beam_rows = frequency * beam_rows
    place_parts, beam_parts = three_parts(pos[...]), three_parts(beam_rows)
    left = jnp.concatenate([part for part in place_parts for _ in range(3)] + [jnp.zeros((8, feeds), jnp.float32)], axis=0)
    right = jnp.concatenate(beam_parts * 3 + [jnp.zeros((8, LANES), jnp.float32)], axis=0)
    turns = lax.dot_general(left.astype(jnp.bfloat16), right.astype(jnp.bfloat16), (((0,), (0,)), ((), ())), preferred_element_type=jnp.float32)
    cosine[...], sine[...] = cos_sin_turns(turns)
    scale_columns = jnp.transpose(scales[...].astype(jnp.float32)).astype(jnp.bfloat16)

    window = volt.shape[3]
    for c in range(CHANS):
        if c in edges:
            in_first_block(blocks, copies[edges.index(c)].wait)

        product = channel_product(volt, c, scale_columns, cosine, sine, window, feeds)
        half = 2 * window
        real = product[:half, :LANES] - product[half:, LANES:]
        imag = product[:half, LANES:] + product[half:, :LANES]
        both = real * real + imag * imag
        detected = both[:window] + both[window:]
        flat = detected - jnp.mean(detected, axis=0, keepdims=True)
        power[pl.ds(c, window, stride=CHANS), :] = flat

    for octet in range(window // OCTET):
        tiles = [power[(octet * OCTET + t) * CHANS : (octet * OCTET + t + 1) * CHANS, :] for t in range(OCTET)]
        tiles = swap_lanes_and_list([tile.astype(jnp.bfloat16) for tile in tiles], CHANS)
        for h in range(OCTET):
            out_ref[0, h, octet * CHANS : (octet + 1) * CHANS, :] = tiles[h]
            if octet >= 2:
                out_ref[1, h, (octet - 2) * CHANS : (octet - 1) * CHANS, :] = tiles[h]
    for h in range(OCTET):
        out_ref[1, h, 2 * CHANS :, :] = jnp.zeros((2 * CHANS, LANES), jnp.bfloat16)


def beams(voltages, scales, feed_positions, beam_directions, dm_trials, chan_total):
    window, feeds = voltages.shape[3:]
    beam_count = beam_directions.shape[1]
    blocks = beam_count // LANES
    trials = dm_trials.shape[0]
    divisor = trials * 192 // (MAXD + 1)
    inputs = (voltages, scales, feed_positions, beam_directions, dm_trials[None, :])
    return pl.pallas_call(
        functools.partial(beam_kernel, chan_total, blocks, divisor),
        grid=(blocks,),
        in_specs=[pl.BlockSpec(memory_space=pl.ANY)] * len(inputs),
        out_specs=(
            pl.BlockSpec((2, OCTET, 4 * CHANS, LANES), lambda i: (0, i, 0, 0)),
            pl.BlockSpec((trials, chan_total), lambda i: (0, 0)),
        ),
        out_shape=(
            jax.ShapeDtypeStruct((2, blocks * OCTET, 4 * CHANS, LANES), jnp.bfloat16),
            jax.ShapeDtypeStruct((trials, chan_total), jnp.float32),
        ),
        scratch_shapes=[
            pltpu.VMEM(voltages.shape, jnp.int32),
            pltpu.VMEM(scales.shape, jnp.int32),
            pltpu.VMEM(feed_positions.shape, jnp.float32),
            pltpu.VMEM(beam_directions.shape, jnp.float32),
            pltpu.VMEM((1, trials), jnp.int32),
            pltpu.VMEM((feeds, LANES), jnp.float32),
            pltpu.VMEM((feeds, LANES), jnp.float32),
            pltpu.VMEM((window * CHANS, LANES), jnp.float32),
            pltpu.SemaphoreType.DMA((len(BATCHES),)),
            pltpu.SemaphoreType.DMA((len(inputs) - 1,)),
        ],
        compiler_params=pltpu.CompilerParams(vmem_limit_bytes=BEAM_VMEM),
        name="beams",
    )(*(pltpu.with_memory_space_constraint(x, pltpu.HBM) for x in inputs))


def dedisperse_kernel(scaling, parts, arrived_ref, delays_ref, out_hbm, total, sem):
    part = pl.program_id(0)
    depth = arrived_ref.shape[0] * CHANS
    delays = delays_ref[...]
    tiles = [arrived_ref[:, o * CHANS : (o + 1) * CHANS, :].reshape(depth, LANES) for o in range(4)]
    lane = lax.broadcasted_iota(jnp.int32, (depth, LANES), 1)
    summed = None
    for r in range(OCTET):
        if r == 0:
            moved = tiles[:3]
        else:
            rolled = [pltpu.roll(tile, LANES - r * CHANS, 1) for tile in tiles]
            moved = [jnp.where(lane < LANES - r * CHANS, rolled[o], rolled[o + 1]) for o in range(3)]
        for a in range(2):
            mask = jnp.where(delays == OCTET * a + r, 1.0, 0.0).astype(jnp.bfloat16)
            piece = jnp.concatenate([moved[a], moved[a + 1]], axis=1)
            product = jnp.dot(mask, piece, preferred_element_type=jnp.float32)
            summed = product if summed is None else summed + product
    summed = summed * scaling
    if parts == 1:
        total[...] = summed
    else:
        total[...] = jnp.where(part == 0, 0.0, total[...]) + summed

    def leave():
        copy = pltpu.make_async_copy(total, out_hbm.at[:, 0, :], sem)
        copy.start()
        copy.wait()

    if parts == 1:
        leave()
    else:
        pl.when(part == parts - 1)(leave)


def dedisperse(arrived, delays):
    sources = arrived.shape[0]
    trials, chan_total = delays.shape
    group = min(sources, 16)
    depth = group * CHANS
    scaling = POWER_SCALE / math.sqrt(chan_total)
    return pl.pallas_call(
        functools.partial(dedisperse_kernel, scaling, sources // group),
        grid=(sources // group,),
        in_specs=[
            pl.BlockSpec((group, 4 * CHANS, LANES), lambda i: (i, 0, 0)),
            pl.BlockSpec((trials, depth), lambda i: (0, i)),
        ],
        out_specs=pl.BlockSpec(memory_space=pl.ANY),
        out_shape=jax.ShapeDtypeStruct((trials, 1, 2 * LANES), jnp.float32),
        scratch_shapes=[
            pltpu.VMEM((trials, 2 * LANES), jnp.float32),
            pltpu.SemaphoreType.DMA(()),
        ],
        compiler_params=pltpu.CompilerParams(vmem_limit_bytes=VMEM_LIMIT),
        name="dedisperse",
    )(arrived, delays)


def local(voltages, scales, feed_positions, beam_directions, dm_trials):
    groups = lax.axis_size("chan")
    chan_total = groups * voltages.shape[0]
    outgoing, delays = beams(voltages, scales, feed_positions, beam_directions, dm_trials, chan_total)
    outgoing = outgoing.reshape(groups, 4 * CHANS, LANES)
    arrived = lax.all_to_all(outgoing, "chan", split_axis=0, concat_axis=0, tiled=True)
    return dedisperse(arrived, delays)


def solution(mesh):
    return jax.shard_map(
        local,
        mesh=mesh,
        in_specs=(
            P(("grp", "chan"), None, None, None, None),
            P(("grp", "chan"), None),
            P(),
            P(),
            P(),
        ),
        out_specs=P(None, ("grp", "chan"), None),
        check_vma=False,
    )
```

```python
import functools
import math

import jax
import jax.numpy as jnp
from jax import lax
from jax.experimental import pallas as pl
from jax.experimental.pallas import tpu as pltpu
from jax.sharding import PartitionSpec as P

MAXD = 15
POWER_SCALE = 1.0 / 67108864.0
LANES = 128
CHANS = 16
OCTET = 8
BATCHES = (4, 4, 4, 4)
DEPTH = 1024
BEAM_VMEM = 40 * 1024 * 1024
VMEM_LIMIT = 24 * 1024 * 1024

SIN_TERMS = (6.283184916, -41.34158923, 81.59994333, -76.61447253, 41.34288235, -12.47124353)
COS_TERMS = (0.9999999891, -19.7392045, 64.93911746, -85.45013953, 60.16763095, -25.96759925, 6.528658158)


def horner(terms, square):
    total = jnp.full_like(square, terms[-1])
    for term in terms[-2::-1]:
        total = total * square + jnp.float32(term)
    return total


def cos_sin_turns(turns):
    rest = turns - jnp.round(turns)
    square = rest * rest
    return horner(COS_TERMS, square), horner(SIN_TERMS, square) * rest


def swap_lanes_and_list(tiles, width):
    count = len(tiles)
    lane = lax.broadcasted_iota(jnp.int32, tiles[0].shape, 1)
    tiles = list(tiles)
    step = count // 2
    while step >= 1:
        upper = ((lane // (step * width)) & 1) == 1
        for low in range(count):
            if low & step:
                continue
            a, b = tiles[low], tiles[low + step]
            tiles[low] = jnp.where(upper, pltpu.roll(b, step * width, 1), a)
            tiles[low + step] = jnp.where(upper, b, pltpu.roll(a, LANES - step * width, 1))
        step //= 2
    return tiles


def keep_power(c, product, power, window):
    half = 2 * window
    real = product[:half, :LANES] - product[half:, LANES:]
    imag = product[:half, LANES:] + product[half:, :LANES]
    both = real * real + imag * imag
    detected = both[:window] + both[window:]
    flat = detected - jnp.mean(detected, axis=0, keepdims=True)
    power[pl.ds(c, window, stride=CHANS), :] = flat


def in_first_block(blocks, action):
    if blocks == 1:
        action()
    else:
        pl.when(pl.program_id(0) == 0)(action)


def channel_product(volt, c, scale_columns, cosine, sine, window, feeds):
    total = None
    for low in range(0, feeds, DEPTH):
        at = slice(low, low + DEPTH)
        rows = volt[c, :, :, :, at].reshape(4 * window, DEPTH).astype(jnp.float32).astype(jnp.bfloat16)
        scale = jnp.broadcast_to(scale_columns[at, c : c + 1], (DEPTH, LANES)).astype(jnp.float32)
        weights = jnp.concatenate([(scale * cosine[at, :]).astype(jnp.bfloat16), (scale * sine[at, :]).astype(jnp.bfloat16)], axis=1)
        part = jnp.dot(rows, weights, preferred_element_type=jnp.float32)
        total = part if total is None else total + part
    return total


def three_parts(rows):
    rest = jnp.concatenate([rows, jnp.zeros((5, rows.shape[1]), jnp.float32)], axis=0)
    parts = []
    for _ in range(3):
        parts.append(rest.astype(jnp.bfloat16).astype(jnp.float32))
        rest = rest - parts[-1]
    return parts


def write_delays(divisor, dm, delays_ref):
    trials, chan_total = delays_ref.shape
    upper = chan_total + lax.broadcasted_iota(jnp.int32, (1, chan_total), 1)
    sweeps = ((256 * chan_total * chan_total) // (upper * upper) - 64).astype(jnp.float32)
    column = jnp.transpose(jnp.broadcast_to(dm[...].astype(jnp.float32), (8, trials)))[:, 0:1]
    delays_ref[...] = jnp.floor((column * sweeps + 0.5) * (1.0 / divisor))


def beam_kernel(chan_total, blocks, divisor, volt_hbm, scales_hbm, pos_hbm, dirs_hbm, dm_hbm, out_ref, delays_ref, volt, scales, pos, dirs, dm, cosine, sine, power, sems, small_sems):
    edges = [sum(BATCHES[:k]) for k in range(len(BATCHES) + 1)]
    small = [
        pltpu.make_async_copy(source, target, small_sems.at[k])
        for k, (source, target) in enumerate(((pos_hbm, pos), (dirs_hbm, dirs), (scales_hbm, scales), (dm_hbm, dm)))
    ]
    copies = [
        pltpu.make_async_copy(volt_hbm.at[low:high], volt.at[low:high], sems.at[k])
        for k, (low, high) in enumerate(zip(edges, edges[1:]))
    ]

    def start_all():
        for copy in small:
            copy.start(priority=0)
        for copy in copies:
            copy.start(priority=1)
        for copy in small:
            copy.wait()

    in_first_block(blocks, start_all)

    in_first_block(blocks, lambda: write_delays(divisor, dm, delays_ref))
    first_chan = lax.axis_index("chan") * CHANS
    frequency = first_chan.astype(jnp.float32) / chan_total + 1.0
    feeds = pos.shape[1]
    if blocks == 1:
        beam_rows = dirs[...]
    else:
        beam_rows = dirs[:, pl.ds(pl.multiple_of(pl.program_id(0) * LANES, LANES), LANES)]
    beam_rows = frequency * beam_rows
    place_parts, beam_parts = three_parts(pos[...]), three_parts(beam_rows)
    left = jnp.concatenate([part for part in place_parts for _ in range(3)] + [jnp.zeros((8, feeds), jnp.float32)], axis=0)
    right = jnp.concatenate(beam_parts * 3 + [jnp.zeros((8, LANES), jnp.float32)], axis=0)
    turns = lax.dot_general(left.astype(jnp.bfloat16), right.astype(jnp.bfloat16), (((0,), (0,)), ((), ())), preferred_element_type=jnp.float32)
    cosine[...], sine[...] = cos_sin_turns(turns)
    scale_columns = jnp.transpose(scales[...].astype(jnp.float32)).astype(jnp.bfloat16)

    window = volt.shape[3]
    held = None
    for c in range(CHANS):
        if c in edges:
            in_first_block(blocks, copies[edges.index(c)].wait)

        product = channel_product(volt, c, scale_columns, cosine, sine, window, feeds)
        if held is not None:
            keep_power(c - 1, held, power, window)
        held = product
    keep_power(CHANS - 1, held, power, window)

    for octet in range(window // OCTET):
        tiles = [power[(octet * OCTET + t) * CHANS : (octet * OCTET + t + 1) * CHANS, :] for t in range(OCTET)]
        tiles = swap_lanes_and_list([tile.astype(jnp.bfloat16) for tile in tiles], CHANS)
        for h in range(OCTET):
            out_ref[0, h, octet * CHANS : (octet + 1) * CHANS, :] = tiles[h]
            if octet >= 2:
                out_ref[1, h, (octet - 2) * CHANS : (octet - 1) * CHANS, :] = tiles[h]
    for h in range(OCTET):
        out_ref[1, h, 2 * CHANS :, :] = jnp.zeros((2 * CHANS, LANES), jnp.bfloat16)


def beams(voltages, scales, feed_positions, beam_directions, dm_trials, chan_total):
    window, feeds = voltages.shape[3:]
    beam_count = beam_directions.shape[1]
    blocks = beam_count // LANES
    trials = dm_trials.shape[0]
    divisor = trials * 192 // (MAXD + 1)
    inputs = (voltages, scales, feed_positions, beam_directions, dm_trials[None, :])
    return pl.pallas_call(
        functools.partial(beam_kernel, chan_total, blocks, divisor),
        grid=(blocks,),
        in_specs=[pl.BlockSpec(memory_space=pl.ANY)] * len(inputs),
        out_specs=(
            pl.BlockSpec((2, OCTET, 4 * CHANS, LANES), lambda i: (0, i, 0, 0)),
            pl.BlockSpec((trials, chan_total), lambda i: (0, 0)),
        ),
        out_shape=(
            jax.ShapeDtypeStruct((2, blocks * OCTET, 4 * CHANS, LANES), jnp.bfloat16),
            jax.ShapeDtypeStruct((trials, chan_total), jnp.float32),
        ),
        scratch_shapes=[
            pltpu.VMEM(voltages.shape, jnp.int32),
            pltpu.VMEM(scales.shape, jnp.int32),
            pltpu.VMEM(feed_positions.shape, jnp.float32),
            pltpu.VMEM(beam_directions.shape, jnp.float32),
            pltpu.VMEM((1, trials), jnp.int32),
            pltpu.VMEM((feeds, LANES), jnp.float32),
            pltpu.VMEM((feeds, LANES), jnp.float32),
            pltpu.VMEM((window * CHANS, LANES), jnp.float32),
            pltpu.SemaphoreType.DMA((len(BATCHES),)),
            pltpu.SemaphoreType.DMA((len(inputs) - 1,)),
        ],
        compiler_params=pltpu.CompilerParams(vmem_limit_bytes=BEAM_VMEM),
        name="beams",
    )(*(pltpu.with_memory_space_constraint(x, pltpu.HBM) for x in inputs))


def dedisperse_kernel(scaling, parts, arrived_ref, delays_ref, out_hbm, total, sem):
    part = pl.program_id(0)
    depth = arrived_ref.shape[0] * CHANS
    delays = delays_ref[...]
    tiles = [arrived_ref[:, o * CHANS : (o + 1) * CHANS, :].reshape(depth, LANES) for o in range(4)]
    lane = lax.broadcasted_iota(jnp.int32, (depth, LANES), 1)
    summed = None
    for r in range(OCTET):
        if r == 0:
            moved = tiles[:3]
        else:
            rolled = [pltpu.roll(tile, LANES - r * CHANS, 1) for tile in tiles]
            moved = [jnp.where(lane < LANES - r * CHANS, rolled[o], rolled[o + 1]) for o in range(3)]
        for a in range(2):
            mask = jnp.where(delays == OCTET * a + r, 1.0, 0.0).astype(jnp.bfloat16)
            piece = jnp.concatenate([moved[a], moved[a + 1]], axis=1)
            product = jnp.dot(mask, piece, preferred_element_type=jnp.float32)
            summed = product if summed is None else summed + product
    summed = summed * scaling
    if parts == 1:
        total[...] = summed
    else:
        total[...] = jnp.where(part == 0, 0.0, total[...]) + summed

    def leave():
        copy = pltpu.make_async_copy(total, out_hbm.at[:, 0, :], sem)
        copy.start()
        copy.wait()

    if parts == 1:
        leave()
    else:
        pl.when(part == parts - 1)(leave)


def dedisperse(arrived, delays):
    sources = arrived.shape[0]
    trials, chan_total = delays.shape
    group = min(sources, 16)
    depth = group * CHANS
    scaling = POWER_SCALE / math.sqrt(chan_total)
    return pl.pallas_call(
        functools.partial(dedisperse_kernel, scaling, sources // group),
        grid=(sources // group,),
        in_specs=[
            pl.BlockSpec((group, 4 * CHANS, LANES), lambda i: (i, 0, 0)),
            pl.BlockSpec((trials, depth), lambda i: (0, i)),
        ],
        out_specs=pl.BlockSpec(memory_space=pl.ANY),
        out_shape=jax.ShapeDtypeStruct((trials, 1, 2 * LANES), jnp.float32),
        scratch_shapes=[
            pltpu.VMEM((trials, 2 * LANES), jnp.float32),
            pltpu.SemaphoreType.DMA(()),
        ],
        compiler_params=pltpu.CompilerParams(vmem_limit_bytes=VMEM_LIMIT),
        name="dedisperse",
    )(arrived, delays)


def local(voltages, scales, feed_positions, beam_directions, dm_trials):
    groups = lax.axis_size("chan")
    chan_total = groups * voltages.shape[0]
    outgoing, delays = beams(voltages, scales, feed_positions, beam_directions, dm_trials, chan_total)
    outgoing = outgoing.reshape(groups, 4 * CHANS, LANES)
    arrived = lax.all_to_all(outgoing, "chan", split_axis=0, concat_axis=0, tiled=True)
    return dedisperse(arrived, delays)


def solution(mesh):
    return jax.shard_map(
        local,
        mesh=mesh,
        in_specs=(
            P(("grp", "chan"), None, None, None, None),
            P(("grp", "chan"), None),
            P(),
            P(),
            P(),
        ),
        out_specs=P(None, ("grp", "chan"), None),
        check_vma=False,
    )
```

```python
import functools
import math

import jax
import jax.numpy as jnp
from jax import lax
from jax.experimental import pallas as pl
from jax.experimental.pallas import tpu as pltpu
from jax.sharding import PartitionSpec as P

MAXD = 15
POWER_SCALE = 1.0 / 67108864.0
LANES = 128
CHANS = 16
OCTET = 8
BATCHES = (4, 4, 4, 4)
DEPTH = 1024
BEAM_VMEM = 40 * 1024 * 1024
VMEM_LIMIT = 24 * 1024 * 1024

SIN_TERMS = (6.283184916, -41.34158923, 81.59994333, -76.61447253, 41.34288235, -12.47124353)
COS_TERMS = (0.9999999891, -19.7392045, 64.93911746, -85.45013953, 60.16763095, -25.96759925, 6.528658158)


def horner(terms, square):
    total = jnp.full_like(square, terms[-1])
    for term in terms[-2::-1]:
        total = total * square + jnp.float32(term)
    return total


def cos_sin_turns(turns):
    rest = turns - jnp.round(turns)
    square = rest * rest
    return horner(COS_TERMS, square), horner(SIN_TERMS, square) * rest


def swap_lanes_and_list(tiles, width):
    count = len(tiles)
    lane = lax.broadcasted_iota(jnp.int32, tiles[0].shape, 1)
    tiles = list(tiles)
    step = count // 2
    while step >= 1:
        upper = ((lane // (step * width)) & 1) == 1
        for low in range(count):
            if low & step:
                continue
            a, b = tiles[low], tiles[low + step]
            tiles[low] = jnp.where(upper, pltpu.roll(b, step * width, 1), a)
            tiles[low + step] = jnp.where(upper, b, pltpu.roll(a, LANES - step * width, 1))
        step //= 2
    return tiles


def keep_power(c, product, power, window):
    half = 2 * window
    real = product[:half, :LANES] - product[half:, LANES:]
    imag = product[:half, LANES:] + product[half:, :LANES]
    both = real * real + imag * imag
    detected = both[:window] + both[window:]
    flat = detected - jnp.mean(detected, axis=0, keepdims=True)
    power[pl.ds(c, window, stride=CHANS), :] = flat


def in_first_block(blocks, action):
    if blocks == 1:
        action()
    else:
        pl.when(pl.program_id(0) == 0)(action)


def channel_product(volt, c, scale_columns, cosine, sine, window, feeds):
    total = None
    for low in range(0, feeds, DEPTH):
        at = slice(low, low + DEPTH)
        rows = volt[c, :, :, :, at].reshape(4 * window, DEPTH).astype(jnp.bfloat16)
        scale = jnp.broadcast_to(scale_columns[at, c : c + 1], (DEPTH, LANES)).astype(jnp.float32)
        weights = jnp.concatenate([(scale * cosine[at, :]).astype(jnp.bfloat16), (scale * sine[at, :]).astype(jnp.bfloat16)], axis=1)
        part = jnp.dot(rows, weights, preferred_element_type=jnp.float32)
        total = part if total is None else total + part
    return total


def three_parts(rows):
    rest = jnp.concatenate([rows, jnp.zeros((5, rows.shape[1]), jnp.float32)], axis=0)
    parts = []
    for _ in range(3):
        parts.append(rest.astype(jnp.bfloat16).astype(jnp.float32))
        rest = rest - parts[-1]
    return parts


def write_delays(divisor, dm, delays_ref):
    trials, chan_total = delays_ref.shape
    upper = chan_total + lax.broadcasted_iota(jnp.int32, (1, chan_total), 1)
    sweeps = ((256 * chan_total * chan_total) // (upper * upper) - 64).astype(jnp.float32)
    column = jnp.transpose(jnp.broadcast_to(dm[...].astype(jnp.float32), (8, trials)))[:, 0:1]
    delays_ref[...] = jnp.floor((column * sweeps + 0.5) * (1.0 / divisor))


def beam_kernel(chan_total, blocks, divisor, volt_hbm, scales_hbm, pos_hbm, dirs_hbm, dm_hbm, out_ref, delays_ref, volt, scales, pos, dirs, dm, cosine, sine, power, sems, small_sems):
    edges = [sum(BATCHES[:k]) for k in range(len(BATCHES) + 1)]
    small = [
        pltpu.make_async_copy(source, target, small_sems.at[k])
        for k, (source, target) in enumerate(((pos_hbm, pos), (dirs_hbm, dirs), (scales_hbm, scales), (dm_hbm, dm)))
    ]
    copies = [
        pltpu.make_async_copy(volt_hbm.at[low:high], volt.at[low:high], sems.at[k])
        for k, (low, high) in enumerate(zip(edges, edges[1:]))
    ]

    def start_all():
        for copy in small:
            copy.start(priority=0)
        for copy in copies:
            copy.start(priority=1)
        for copy in small:
            copy.wait()

    in_first_block(blocks, start_all)

    in_first_block(blocks, lambda: write_delays(divisor, dm, delays_ref))
    first_chan = lax.axis_index("chan") * CHANS
    frequency = first_chan.astype(jnp.float32) / chan_total + 1.0
    feeds = pos.shape[1]
    if blocks == 1:
        beam_rows = dirs[...]
    else:
        beam_rows = dirs[:, pl.ds(pl.multiple_of(pl.program_id(0) * LANES, LANES), LANES)]
    beam_rows = frequency * beam_rows
    place_parts, beam_parts = three_parts(pos[...]), three_parts(beam_rows)
    left = jnp.concatenate([part for part in place_parts for _ in range(3)] + [jnp.zeros((8, feeds), jnp.float32)], axis=0)
    right = jnp.concatenate(beam_parts * 3 + [jnp.zeros((8, LANES), jnp.float32)], axis=0)
    turns = lax.dot_general(left.astype(jnp.bfloat16), right.astype(jnp.bfloat16), (((0,), (0,)), ((), ())), preferred_element_type=jnp.float32)
    cosine[...], sine[...] = cos_sin_turns(turns)
    scale_columns = jnp.transpose(scales[...].astype(jnp.float32)).astype(jnp.bfloat16)

    window = volt.shape[3]
    held = None
    for c in range(CHANS):
        if c in edges:
            in_first_block(blocks, copies[edges.index(c)].wait)

        product = channel_product(volt, c, scale_columns, cosine, sine, window, feeds)
        if held is not None:
            keep_power(c - 1, held, power, window)
        held = product
    keep_power(CHANS - 1, held, power, window)

    for octet in range(window // OCTET):
        tiles = [power[(octet * OCTET + t) * CHANS : (octet * OCTET + t + 1) * CHANS, :] for t in range(OCTET)]
        tiles = swap_lanes_and_list([tile.astype(jnp.bfloat16) for tile in tiles], CHANS)
        for h in range(OCTET):
            out_ref[0, h, octet * CHANS : (octet + 1) * CHANS, :] = tiles[h]
            if octet >= 2:
                out_ref[1, h, (octet - 2) * CHANS : (octet - 1) * CHANS, :] = tiles[h]
    for h in range(OCTET):
        out_ref[1, h, 2 * CHANS :, :] = jnp.zeros((2 * CHANS, LANES), jnp.bfloat16)


def beams(voltages, scales, feed_positions, beam_directions, dm_trials, chan_total):
    window, feeds = voltages.shape[3:]
    beam_count = beam_directions.shape[1]
    blocks = beam_count // LANES
    trials = dm_trials.shape[0]
    divisor = trials * 192 // (MAXD + 1)
    inputs = (voltages, scales, feed_positions, beam_directions, dm_trials[None, :])
    return pl.pallas_call(
        functools.partial(beam_kernel, chan_total, blocks, divisor),
        grid=(blocks,),
        in_specs=[pl.BlockSpec(memory_space=pl.ANY)] * len(inputs),
        out_specs=(
            pl.BlockSpec((2, OCTET, 4 * CHANS, LANES), lambda i: (0, i, 0, 0)),
            pl.BlockSpec((trials, chan_total), lambda i: (0, 0)),
        ),
        out_shape=(
            jax.ShapeDtypeStruct((2, blocks * OCTET, 4 * CHANS, LANES), jnp.bfloat16),
            jax.ShapeDtypeStruct((trials, chan_total), jnp.float32),
        ),
        scratch_shapes=[
            pltpu.VMEM(voltages.shape, jnp.int32),
            pltpu.VMEM(scales.shape, jnp.int32),
            pltpu.VMEM(feed_positions.shape, jnp.float32),
            pltpu.VMEM(beam_directions.shape, jnp.float32),
            pltpu.VMEM((1, trials), jnp.int32),
            pltpu.VMEM((feeds, LANES), jnp.float32),
            pltpu.VMEM((feeds, LANES), jnp.float32),
            pltpu.VMEM((window * CHANS, LANES), jnp.float32),
            pltpu.SemaphoreType.DMA((len(BATCHES),)),
            pltpu.SemaphoreType.DMA((len(inputs) - 1,)),
        ],
        compiler_params=pltpu.CompilerParams(vmem_limit_bytes=BEAM_VMEM),
        name="beams",
    )(*(pltpu.with_memory_space_constraint(x, pltpu.HBM) for x in inputs))


def dedisperse_kernel(scaling, parts, arrived_ref, delays_ref, out_hbm, total, sem):
    part = pl.program_id(0)
    depth = arrived_ref.shape[0] * CHANS
    delays = delays_ref[...]
    tiles = [arrived_ref[:, o * CHANS : (o + 1) * CHANS, :].reshape(depth, LANES) for o in range(4)]
    lane = lax.broadcasted_iota(jnp.int32, (depth, LANES), 1)
    summed = None
    for r in range(OCTET):
        if r == 0:
            moved = tiles[:3]
        else:
            rolled = [pltpu.roll(tile, LANES - r * CHANS, 1) for tile in tiles]
            moved = [jnp.where(lane < LANES - r * CHANS, rolled[o], rolled[o + 1]) for o in range(3)]
        for a in range(2):
            mask = jnp.where(delays == OCTET * a + r, 1.0, 0.0).astype(jnp.bfloat16)
            piece = jnp.concatenate([moved[a], moved[a + 1]], axis=1)
            product = jnp.dot(mask, piece, preferred_element_type=jnp.float32)
            summed = product if summed is None else summed + product
    summed = summed * scaling
    if parts == 1:
        total[...] = summed
    else:
        total[...] = jnp.where(part == 0, 0.0, total[...]) + summed

    def leave():
        sides = [
            pltpu.make_async_copy(total.at[:, at], out_hbm.at[:, 0, at], sem.at[k])
            for k, at in enumerate((slice(0, LANES), slice(LANES, 2 * LANES)))
        ]
        for copy in sides:
            copy.start()
        for copy in sides:
            copy.wait()

    if parts == 1:
        leave()
    else:
        pl.when(part == parts - 1)(leave)


def dedisperse(arrived, delays):
    sources = arrived.shape[0]
    trials, chan_total = delays.shape
    group = min(sources, 16)
    depth = group * CHANS
    scaling = POWER_SCALE / math.sqrt(chan_total)
    return pl.pallas_call(
        functools.partial(dedisperse_kernel, scaling, sources // group),
        grid=(sources // group,),
        in_specs=[
            pl.BlockSpec((group, 4 * CHANS, LANES), lambda i: (i, 0, 0)),
            pl.BlockSpec((trials, depth), lambda i: (0, i)),
        ],
        out_specs=pl.BlockSpec(memory_space=pl.ANY),
        out_shape=jax.ShapeDtypeStruct((trials, 1, 2 * LANES), jnp.float32),
        scratch_shapes=[
            pltpu.VMEM((trials, 2 * LANES), jnp.float32),
            pltpu.SemaphoreType.DMA((2,)),
        ],
        compiler_params=pltpu.CompilerParams(vmem_limit_bytes=VMEM_LIMIT),
        name="dedisperse",
    )(arrived, delays)


def local(voltages, scales, feed_positions, beam_directions, dm_trials):
    groups = lax.axis_size("chan")
    chan_total = groups * voltages.shape[0]
    outgoing, delays = beams(voltages, scales, feed_positions, beam_directions, dm_trials, chan_total)
    outgoing = outgoing.reshape(groups, 4 * CHANS, LANES)
    arrived = lax.all_to_all(outgoing, "chan", split_axis=0, concat_axis=0, tiled=True)
    return dedisperse(arrived, delays)


def solution(mesh):
    return jax.shard_map(
        local,
        mesh=mesh,
        in_specs=(
            P(("grp", "chan"), None, None, None, None),
            P(("grp", "chan"), None),
            P(),
            P(),
            P(),
        ),
        out_specs=P(None, ("grp", "chan"), None),
        check_vma=False,
    )
```
